32 devices in a mesh: parts: 2 (over x), dom: 8 (over z, y), grp: 2 (over core).
Axes of the slice: x: 2, y: 2, z: 4, core: 2. Of those that a mesh axis runs over, the one named last changes fastest.
Arguments:
- basis: bfloat16 [49152, 768], P(('parts', 'dom', 'grp')), parts along dimension 0, may hold values from -6 to 6
- blocks: bfloat16 [9, 16, 49152], P(None, None, ('parts', 'dom', 'grp')), parts along dimension 2, may hold values from -0.0034179688 to 0.0034179688
- columns: int32 [16, 49152], P(None, ('parts', 'dom', 'grp')), parts along dimension 1, may hold values from 0 to 2015, as said below
- send_list: int32 [32, 6, 80], P(('parts', 'dom', 'grp')), parts along dimension 0, may hold values from 0 to 1535
- send_counts: int32 [32, 6], P(('parts', 'dom', 'grp')), parts along dimension 0, may hold values from 20 to 80, as said below
Outputs:
- reduced_stiffness: float32 [512, 256], P(('parts', 'dom')), parts along dimension 0
The draws below stay inside these ranges and needn't reach their ends.
There are 2 independent parts, one for each index of `parts`. The reference program is written for one: setup_inputs(seed, part) draws one part's arguments, and reference() takes and returns one part's arrays. A program takes and returns all parts, laid end to end along the dimension named above; each array names one. Nothing has to cross between parts.
Inputs may be any that keep to these rules, and one draw needn't show every extreme that they name: `send_counts`: in every draw, within each node group, one partition receives 80 live slots from each of its 6 neighbours. `columns`: block slots of a partition's first 1152 nodes name owned nodes only; the others name owned nodes or live ghost slots.
All inputs are finite; a program needn't handle non-finite values.
Results may differ from the reference program's by a relative error of at most 0.0029.
Values may be sent and summed in bfloat16 or wider, within the bound.
A program may use at most 128 MiB of HBM per device.

```python
import jax
import jax.numpy as jnp
from jax import lax

R = 256
NNZ = 16
NODE_DEV = 1536
GHOST_CAP = 80
REACH = 3
EDGE = 384
NODES = 24576
N_DOM = 8
N_GRP = 2


def neighbour_offsets():
    index = jnp.arange(2 * REACH, dtype=jnp.int32)
    lower = jnp.where(index < REACH - 1, index + 1, N_DOM // 2)
    upper = jnp.where(index < 2 * REACH - 1, -(index - REACH + 1), N_DOM // 2 + 1)
    return jnp.where(index < REACH, lower, upper).astype(jnp.int32)


def shared_counts(key):
    first_key = jax.random.fold_in(key, 101)
    second_key = jax.random.fold_in(key, 102)
    total = N_DOM * N_GRP
    counts = jax.random.randint(first_key, (total, 2 * REACH), GHOST_CAP // 4, GHOST_CAP + 1)
    target = jax.random.randint(second_key, (N_GRP,), 0, N_DOM)
    senders = jnp.arange(total, dtype=jnp.int32) // N_GRP
    groups = jnp.arange(total, dtype=jnp.int32) % N_GRP
    dest = (senders[:, None] + neighbour_offsets()[None, :]) % N_DOM
    filled = dest == target[groups][:, None]
    counts = jnp.where(filled, GHOST_CAP, counts).astype(jnp.int32)
    return (counts, target)


def draw_send_counts(key, part):
    counts, target = shared_counts(key)
    return counts


def draw_columns(key, part):
    counts, target = shared_counts(key)
    key = jax.random.fold_in(key, 23)
    total = N_DOM * N_GRP
    neighbours = 2 * REACH
    within = jnp.arange(total, dtype=jnp.int32) // N_GRP
    groups = jnp.arange(total, dtype=jnp.int32) % N_GRP
    offsets = neighbour_offsets()
    sources = (within[:, None] - offsets[None, :]) % N_DOM * N_GRP + groups[:, None]
    incoming = counts[sources, jnp.arange(neighbours, dtype=jnp.int32)[None, :]]
    shape = (NNZ, total, NODE_DEV)
    owned = jax.random.randint(jax.random.fold_in(key, 1), shape, 0, NODE_DEV)
    which = jax.random.randint(jax.random.fold_in(key, 2), shape, 0, neighbours)
    live = incoming[jnp.arange(total, dtype=jnp.int32)[None, :, None], which]
    slot = jax.random.randint(jax.random.fold_in(key, 3), shape, 0, live)
    ghost = NODE_DEV + which * GHOST_CAP + slot
    pick = jax.random.randint(jax.random.fold_in(key, 4), shape, 0, 4) > 0
    edge = (jnp.arange(NODE_DEV, dtype=jnp.int32) >= NODE_DEV - EDGE)[None, None, :]
    cols = jnp.where(jnp.logical_and(edge, pick), ghost, owned)
    is_target = within == target[groups]
    top = NODE_DEV + neighbours * GHOST_CAP - 1
    cols = cols.at[0, :, NODE_DEV - 1].set(jnp.where(is_target, top, cols[0, :, NODE_DEV - 1]))
    return cols.reshape(NNZ, total * NODE_DEV).astype(jnp.int32)


def touch_ends(values, own_key, least, largest):
    spot = [jax.random.randint(jax.random.fold_in(own_key, axis), (), 0, length) for axis, length in enumerate(values.shape)]
    widest = values.shape.index(max(values.shape))
    next_to = spot[:widest] + [(spot[widest] + 1) % values.shape[widest]] + spot[widest + 1:]
    return values.at[tuple(spot)].set(least).at[tuple(next_to)].set(largest)


def level_of(key, extent, shards, least, high):
    def one(dim, shards_of):
        heights = jax.random.uniform(jax.random.fold_in(jax.random.fold_in(key, 6), dim), (shards_of,), jnp.float32, least / len(shards), high / len(shards))
        return jnp.repeat(jnp.exp(heights), extent[dim] // shards_of).reshape((-1,) + (1,) * (len(extent) - dim - 1))

    level = one(*shards[0])
    for cut in shards[1:]:
        level = level * one(*cut)
    return level


def gaussian(stream_key, extent, deviation, bound, shards=(), held_as=jnp.bfloat16):
    values = jax.random.normal(stream_key, extent, jnp.float32) * deviation
    if len(shards) > 0:
        values = level_of(stream_key, extent, shards, -0.22, 0.18) * values
    return jnp.clip(values, min=-bound, max=bound).astype(held_as)


def setup_inputs(seed: int = 0, part: int = 0) -> dict:
    arg_keys = jax.random.split(jax.random.key(seed), 6)
    own_keys = jax.random.split(jax.random.fold_in(arg_keys[5], part), 6)
    basis = gaussian(own_keys[0], (NODES, 3 * R), 1.0, 6.0, ((0, 16),))
    blocks = gaussian(own_keys[1], (9, NNZ, NODES), (9 * NNZ * NODES) ** -0.5, 0.0034179688, ((2, 16),))
    columns = draw_columns(jax.random.fold_in(jax.random.fold_in(arg_keys[5], part), 71), part)
    send_list = touch_ends(jax.random.randint(own_keys[3], (N_DOM * N_GRP, 2 * REACH, GHOST_CAP), 0, NODE_DEV), jax.random.fold_in(own_keys[3], 1), 0, NODE_DEV - 1).astype(jnp.int32)
    send_counts = draw_send_counts(jax.random.fold_in(jax.random.fold_in(arg_keys[5], part), 71), part)
    return {"basis": basis, "blocks": blocks, "columns": columns, "send_list": send_list, "send_counts": send_counts}


def offset_table():
    index = jnp.arange(2 * REACH, dtype=jnp.int32)
    lower = jnp.where(index < REACH - 1, index + 1, N_DOM // 2)
    upper = jnp.where(index < 2 * REACH - 1, -(index - REACH + 1), N_DOM // 2 + 1)
    return jnp.where(index < REACH, lower, upper).astype(jnp.int32)


def reference(basis, blocks, columns, send_list, send_counts):
    parts_total = N_DOM * N_GRP
    neighbours = 2 * REACH
    basis3 = basis.reshape(parts_total, NODE_DEV, 3 * R)
    blocks4 = blocks.reshape(9, NNZ, parts_total, NODE_DEV)
    columns3 = columns.reshape(NNZ, parts_total, NODE_DEV)
    offset_index = jnp.arange(neighbours, dtype=jnp.int32)
    offsets = offset_table()

    def one_partition(total, owner):
        group = owner % N_GRP
        within = owner // N_GRP
        sources = (((within - offsets) % N_DOM) * N_GRP + group).astype(jnp.int32)
        lists = send_list[sources, offset_index]
        counts = send_counts[sources, offset_index]
        ghosts = basis3[sources[:, None], lists]
        live = (jnp.arange(GHOST_CAP, dtype=jnp.int32)[None, :] < counts[:, None])
        ghosts = jnp.where(live[:, :, None], ghosts, jnp.zeros_like(ghosts))
        owned = basis3[owner]
        extended = jnp.concatenate([owned, ghosts.reshape(neighbours * GHOST_CAP, 3 * R)], axis=0)
        own_blocks = blocks4[:, :, owner]
        own_columns = columns3[:, owner]

        def one_slot(slot_index, accum):
            picked = extended[own_columns[slot_index]].reshape(NODE_DEV, 3, R).astype(jnp.float32)
            matrix = own_blocks[:, slot_index].reshape(3, 3, NODE_DEV).astype(jnp.float32)
            return accum + jnp.einsum("abn,nbr->nar", matrix, picked)

        kv_rows = lax.fori_loop(0, NNZ, one_slot, jnp.zeros((NODE_DEV, 3, R), jnp.float32))
        kv_rows = kv_rows.astype(jnp.bfloat16).reshape(NODE_DEV * 3, R)
        left = owned.reshape(NODE_DEV * 3, R)
        term = lax.dot_general(left, kv_rows, (((0,), (0,)), ((), ())), preferred_element_type=jnp.float32)
        return total + term, None

    result, _ = lax.scan(one_partition, jnp.zeros((R, R), jnp.float32), jnp.arange(parts_total, dtype=jnp.int32))
    return result
```

```python
import functools

import jax
import jax.numpy as jnp
from jax import lax
from jax.experimental import pallas as pl
from jax.experimental.pallas import tpu as pltpu
from jax.sharding import PartitionSpec as P

EDGE = 384
TILE = 256
LANES = 128
SUB = 16
F32 = jnp.float32
BF16 = jnp.bfloat16
MESH = pl.DeviceIdType.MESH


def offset_list(neighbours, group_size):
    reach = neighbours // 2
    half_way = group_size // 2
    offsets = [step + 1 for step in range(reach - 1)] + [half_way]
    return offsets + [-(step + 1) for step in range(reach - 1)] + [half_way + 1]


def kernel(
    n, basis_ref, blocks_ref, columns_ref, list_ref, counts_ref, out_ref,
    listpad, picks, outgoing, ghost, colsd, blocksd, wide, rel, kt_a, kt_b, vr, y, term4, sib, summed, landed,
    gsend, grecv, ssend, srecv, rsend, rrecv,
):
    nodes = basis_ref.shape[0]
    width = basis_ref.shape[1] // 3
    nnz = columns_ref.shape[0]
    neighbours, slots = list_ref.shape[1], list_ref.shape[2]
    half_share = sib.shape[1]
    own_tiles = nodes // TILE
    ghost_rows = ghost.shape[0]
    ghost_tiles = ghost_rows // TILE
    parts_me = lax.axis_index("parts")
    me = lax.axis_index("dom")
    grp = lax.axis_index("grp")
    other = 1 - grp
    offsets = offset_list(neighbours, n)

    barrier = pltpu.get_barrier_semaphore()
    pl.semaphore_signal(barrier, inc=1, device_id=(parts_me, me, other), device_id_type=MESH)

    def greet(step, carry):
        to = lax.rem(me + step, n)
        pl.semaphore_signal(barrier, inc=1, device_id=(parts_me, to, 0), device_id_type=MESH)
        pl.semaphore_signal(barrier, inc=1, device_id=(parts_me, to, 1), device_id_type=MESH)
        return carry

    lax.fori_loop(1, n, greet, 0)

    listpad[...] = jnp.full_like(listpad, -1.0)
    lane = lax.broadcasted_iota(jnp.int32, (1, slots), 1)
    for q in range(neighbours):
        row = jnp.where(lane < counts_ref[0, q], list_ref[0, q:q + 1, :], -1)
        listpad[q:q + 1, 0:slots] = row.astype(F32)
    turned = jnp.transpose(listpad[...])
    node_id = lax.broadcasted_iota(jnp.int32, (slots, nodes), 1).astype(F32)
    for q in range(neighbours):
        hit = jnp.broadcast_to(turned[0:slots, q:q + 1], (slots, nodes)) == node_id
        picks[q * slots:(q + 1) * slots, :] = jnp.where(hit, 1.0, 0.0).astype(BF16)
    for piece in range(3):
        cut = slice(piece * width, (piece + 1) * width)
        outgoing[:, cut] = jnp.dot(picks[...], basis_ref[:, cut], preferred_element_type=F32).astype(BF16)
    if ghost_rows > neighbours * slots:
        pad = ghost_rows - neighbours * slots
        ghost[neighbours * slots:, :] = jnp.zeros((pad, 3 * width), BF16)

    pl.semaphore_wait(barrier, 2 * n - 1)

    def ghost_copy(q):
        to = lax.rem(me + (offsets[q] + n), n)
        return pltpu.make_async_remote_copy(
            src_ref=outgoing.at[pl.ds(q * slots, slots)],
            dst_ref=ghost.at[pl.ds(q * slots, slots)],
            send_sem=gsend.at[q],
            recv_sem=grecv.at[q],
            device_id=(parts_me, to, grp),
            device_id_type=MESH,
        )

    for q in range(neighbours):
        ghost_copy(q).start()

    colsd[0:nnz, :] = columns_ref[...]
    colsd[nnz:2 * nnz, :] = columns_ref[...]

    def widen(tile, carry):
        lanes = pl.ds(pl.multiple_of(tile * LANES, LANES), LANES)
        for ab in range(9):
            value = blocks_ref[ab, :, lanes].astype(F32)
            blocksd[ab, 0:nnz, :] = value
            blocksd[ab, nnz:2 * nnz, :] = value
        mine = colsd[0:nnz, lanes]
        sums = [blocksd[ab, 0:nnz, :] for ab in range(9)]
        for shift in range(1, nnz):
            same = mine == colsd[shift:shift + nnz, lanes]
            for ab in range(9):
                sums[ab] = sums[ab] + jnp.where(same, blocksd[ab, shift:shift + nnz, :], 0.0)
        for ab in range(9):
            for slot in range(nnz):
                line = jnp.broadcast_to(sums[ab][slot:slot + 1, :], (SUB, LANES))
                wide[ab, slot, :, lanes] = line.astype(BF16)
        return carry

    lax.fori_loop(0, nodes // LANES, widen, 0)

    for chunk in range(own_tiles):
        for a in range(3):
            vr[chunk, a * TILE:(a + 1) * TILE, :] = basis_ref[
                chunk * TILE:(chunk + 1) * TILE, a * width:(a + 1) * width
            ]

    def clear(tile, carry):
        y[tile] = jnp.zeros((3 * TILE, width), F32)
        return carry

    lax.fori_loop(0, own_tiles + ghost_tiles, clear, 0)
    kt_b[...] = jnp.zeros_like(kt_b)

    base = (
        lax.broadcasted_iota(jnp.int32, (4, SUB, LANES), 0) * SUB
        + lax.broadcasted_iota(jnp.int32, (4, SUB, LANES), 1)
    )

    def build(tile, chunk, kt):
        for part in range(TILE // LANES):
            lanes = pl.ds(pl.multiple_of(chunk * TILE + part * LANES, LANES), LANES)
            near = (columns_ref[:, lanes] - tile * TILE).astype(F32)
            for slot in range(nnz):
                rel[part, slot] = jnp.broadcast_to(near[slot:slot + 1, :], (SUB, LANES)).astype(BF16)
            for quarter in range(4):
                rows = (base + quarter * 4 * SUB).astype(F32).astype(BF16)
                accs = [jnp.zeros((4, SUB, LANES), BF16) for _ in range(9)]
                for slot in range(nnz):
                    hit = jnp.broadcast_to(rel[part, slot][None], (4, SUB, LANES)) == rows
                    for ab in range(9):
                        value = jnp.broadcast_to(wide[ab, slot, :, lanes][None], (4, SUB, LANES))
                        accs[ab] = jnp.where(hit, value, accs[ab])
                for ab in range(9):
                    a, b = ab // 3, ab % 3
                    top = b * TILE + quarter * 4 * SUB
                    left = a * TILE + part * LANES
                    kt[top:top + 4 * SUB, left:left + LANES] = accs[ab].reshape(4 * SUB, LANES)

    def multiply(tile, chunk, kt):
        y[tile] += jnp.dot(kt[...], vr[chunk], preferred_element_type=F32)

    own_pairs = own_tiles // 2
    own_steps = own_tiles * own_pairs
    edge_chunk = (nodes - EDGE) // TILE // 2 * 2
    edge_pairs = (own_tiles - edge_chunk) // 2
    steps = own_steps + ghost_tiles * edge_pairs

    def place(step):
        late = step // own_steps
        tile = (1 - late) * (step // own_pairs) + late * (own_tiles + (step - own_steps) // edge_pairs)
        chunk = (1 - late) * (2 * (step % own_pairs)) + late * (edge_chunk + 2 * (step % edge_pairs))
        return tile, chunk

    def advance(step, carry):
        tile, chunk = place(step)
        tile_before, chunk_before = place((step + steps - 1) % steps)
        build(tile, chunk, kt_a)
        multiply(tile_before, chunk_before + 1, kt_b)
        build(tile, chunk + 1, kt_b)
        multiply(tile, chunk, kt_a)
        return carry

    lax.fori_loop(0, steps, advance, 0)
    tile_last, chunk_last = place(steps - 1)
    multiply(tile_last, chunk_last + 1, kt_b)

    turn = (((0,), (0,)), ((), ()))

    def fold(tile, total):
        return total + lax.dot_general(y[tile].astype(BF16), vr[tile], turn, preferred_element_type=F32)

    total = lax.fori_loop(0, own_tiles, fold, jnp.zeros((width, width), F32))
    for q in range(neighbours):
        ghost_copy(q).wait_recv()
    for tile in range(ghost_tiles):
        for b in range(3):
            total = total + lax.dot_general(
                y[own_tiles + tile, b * TILE:(b + 1) * TILE, :].astype(BF16),
                ghost[tile * TILE:(tile + 1) * TILE, b * width:(b + 1) * width],
                turn,
                preferred_element_type=F32,
            )
    for to in range(n):
        for half in range(2):
            top = (2 * to + half) * half_share
            term4[half, to] = total[top:top + half_share, :]

    pair = pltpu.make_async_remote_copy(
        src_ref=term4.at[other],
        dst_ref=sib,
        send_sem=ssend,
        recv_sem=srecv,
        device_id=(parts_me, me, other),
        device_id_type=MESH,
    )
    pair.start()
    pair.wait_recv()
    summed[...] = term4[grp] + sib[...]

    def share_copy(to, to_grp):
        return pltpu.make_async_remote_copy(
            src_ref=summed.at[to],
            dst_ref=landed.at[grp, me],
            send_sem=rsend.at[to_grp, to],
            recv_sem=rrecv.at[grp, me],
            device_id=(parts_me, to, to_grp),
            device_id_type=MESH,
        )

    def arrival(half, source):
        return pltpu.make_async_remote_copy(
            src_ref=summed.at[source],
            dst_ref=landed.at[half, source],
            send_sem=rsend.at[half, source],
            recv_sem=rrecv.at[half, source],
            device_id=(parts_me, source, half),
            device_id_type=MESH,
        )

    def send(step, carry):
        to = lax.rem(me + step, n)
        share_copy(to, 0).start()
        share_copy(to, 1).start()
        return carry

    lax.fori_loop(1, n, send, 0)
    share_copy(me, other).start()
    landed[grp, me] = summed[me]

    def receive(step, carry):
        source = lax.rem(me + step, n)
        arrival(0, source).wait_recv()
        arrival(1, source).wait_recv()
        return carry

    lax.fori_loop(1, n, receive, 0)
    arrival(other, me).wait_recv()
    for half in range(2):
        out_ref[half * half_share:(half + 1) * half_share, :] = jnp.sum(landed[half], axis=0)

    for q in range(neighbours):
        ghost_copy(q).wait_send()
    pair.wait_send()

    def sent(step, carry):
        to = lax.rem(me + step, n)
        share_copy(to, 0).wait_send()
        share_copy(to, 1).wait_send()
        return carry

    lax.fori_loop(1, n, sent, 0)
    share_copy(me, other).wait_send()


def on_device(basis, blocks, columns, send_list, send_counts):
    nodes, width = basis.shape[0], basis.shape[1] // 3
    nnz = columns.shape[0]
    neighbours, slots = send_list.shape[1], send_list.shape[2]
    n = lax.axis_size("dom")
    share = width // n
    half = share // 2
    own_tiles = nodes // TILE
    ghost_tiles = -(-neighbours * slots // TILE)
    vmem = pl.BlockSpec(memory_space=pltpu.VMEM)
    return pl.pallas_call(
        functools.partial(kernel, n),
        out_shape=jax.ShapeDtypeStruct((share, width), F32),
        in_specs=[vmem, vmem, vmem, vmem, pl.BlockSpec(memory_space=pltpu.SMEM)],
        out_specs=vmem,
        scratch_shapes=[
            pltpu.VMEM((LANES, LANES), F32),
            pltpu.VMEM((neighbours * slots, nodes), BF16),
            pltpu.VMEM((neighbours * slots, 3 * width), BF16),
            pltpu.VMEM((ghost_tiles * TILE, 3 * width), BF16),
            pltpu.VMEM((2 * nnz, nodes), jnp.int32),
            pltpu.VMEM((9, 2 * nnz, LANES), F32),
            pltpu.VMEM((9, nnz, SUB, nodes), BF16),
            pltpu.VMEM((2, nnz, SUB, LANES), BF16),
            pltpu.VMEM((3 * TILE, 3 * TILE), BF16),
            pltpu.VMEM((3 * TILE, 3 * TILE), BF16),
            pltpu.VMEM((own_tiles, 3 * TILE, width), BF16),
            pltpu.VMEM((own_tiles + ghost_tiles, 3 * TILE, width), F32),
            pltpu.VMEM((2, n, half, width), F32),
            pltpu.VMEM((n, half, width), F32),
            pltpu.VMEM((n, half, width), F32),
            pltpu.VMEM((2, n, half, width), F32),
            pltpu.SemaphoreType.DMA((neighbours,)),
            pltpu.SemaphoreType.DMA((neighbours,)),
            pltpu.SemaphoreType.DMA,
            pltpu.SemaphoreType.DMA,
            pltpu.SemaphoreType.DMA((2, n)),
            pltpu.SemaphoreType.DMA((2, n)),
        ],
        compiler_params=pltpu.CompilerParams(
            collective_id=0, has_side_effects=True, vmem_limit_bytes=56 * 1024 * 1024
        ),
    )(basis, blocks, columns, send_list, send_counts)


def solution(mesh):
    in_specs = (
        P(("parts", "dom", "grp"), None),
        P(None, None, ("parts", "dom", "grp")),
        P(None, ("parts", "dom", "grp")),
        P(("parts", "dom", "grp"), None, None),
        P(("parts", "dom", "grp"), None),
    )
    out_specs = P(("parts", "dom"), None)
    return jax.shard_map(
        on_device, mesh=mesh, in_specs=in_specs, out_specs=out_specs, check_vma=False
    )
```

```python
import functools

import jax
import jax.numpy as jnp
from jax import lax
from jax.experimental import pallas as pl
from jax.experimental.pallas import tpu as pltpu
from jax.sharding import PartitionSpec as P

EDGE = 384
TILE = 256
LANES = 128
SUB = 16
F32 = jnp.float32
BF16 = jnp.bfloat16
MESH = pl.DeviceIdType.MESH


def offset_list(neighbours, group_size):
    reach = neighbours // 2
    half_way = group_size // 2
    offsets = [step + 1 for step in range(reach - 1)] + [half_way]
    return offsets + [-(step + 1) for step in range(reach - 1)] + [half_way + 1]


def kernel(
    n, basis_ref, blocks_ref, columns_ref, list_ref, counts_ref, out_ref,
    listpad, picks, outgoing, ghost, colsd, blocksd, wide, rel, kt_a, kt_b, vr, y, term4, sib, summed, landed,
    gsend, grecv, ssend, srecv, rsend, rrecv,
):
    nodes = basis_ref.shape[0]
    width = basis_ref.shape[1] // 3
    nnz = columns_ref.shape[0]
    neighbours, slots = list_ref.shape[1], list_ref.shape[2]
    half_share = sib.shape[1]
    own_tiles = nodes // TILE
    ghost_rows = ghost.shape[0]
    ghost_tiles = ghost_rows // TILE
    parts_me = lax.axis_index("parts")
    me = lax.axis_index("dom")
    grp = lax.axis_index("grp")
    other = 1 - grp
    offsets = offset_list(neighbours, n)

    barrier = pltpu.get_barrier_semaphore()
    pl.semaphore_signal(barrier, inc=1, device_id=(parts_me, me, other), device_id_type=MESH)

    def greet(step, carry):
        to = lax.rem(me + step, n)
        pl.semaphore_signal(barrier, inc=1, device_id=(parts_me, to, 0), device_id_type=MESH)
        pl.semaphore_signal(barrier, inc=1, device_id=(parts_me, to, 1), device_id_type=MESH)
        return carry

    lax.fori_loop(1, n, greet, 0)

    listpad[...] = jnp.full_like(listpad, -1.0)
    lane = lax.broadcasted_iota(jnp.int32, (1, slots), 1)
    for q in range(neighbours):
        row = jnp.where(lane < counts_ref[0, q], list_ref[0, q:q + 1, :], -1)
        listpad[q:q + 1, 0:slots] = row.astype(F32)
    turned = jnp.transpose(listpad[...])
    node_id = lax.broadcasted_iota(jnp.int32, (slots, nodes), 1).astype(F32)
    for q in range(neighbours):
        hit = jnp.broadcast_to(turned[0:slots, q:q + 1], (slots, nodes)) == node_id
        picks[q * slots:(q + 1) * slots, :] = jnp.where(hit, 1.0, 0.0).astype(BF16)
    for piece in range(3):
        cut = slice(piece * width, (piece + 1) * width)
        outgoing[:, cut] = jnp.dot(picks[...], basis_ref[:, cut], preferred_element_type=F32).astype(BF16)
    if ghost_rows > neighbours * slots:
        pad = ghost_rows - neighbours * slots
        ghost[neighbours * slots:, :] = jnp.zeros((pad, 3 * width), BF16)

    pl.semaphore_wait(barrier, 2 * n - 1)

    def ghost_copy(q):
        to = lax.rem(me + (offsets[q] + n), n)
        return pltpu.make_async_remote_copy(
            src_ref=outgoing.at[pl.ds(q * slots, slots)],
            dst_ref=ghost.at[pl.ds(q * slots, slots)],
            send_sem=gsend.at[q],
            recv_sem=grecv.at[q],
            device_id=(parts_me, to, grp),
            device_id_type=MESH,
        )

    for q in range(neighbours):
        ghost_copy(q).start()

    colsd[0:nnz, :] = columns_ref[...]
    colsd[nnz:2 * nnz, :] = columns_ref[...]

    def widen(tile, carry):
        lanes = pl.ds(pl.multiple_of(tile * LANES, LANES), LANES)
        for ab in range(9):
            value = blocks_ref[ab, :, lanes].astype(F32)
            blocksd[ab, 0:nnz, :] = value
            blocksd[ab, nnz:2 * nnz, :] = value
        mine = colsd[0:nnz, lanes]
        sums = [blocksd[ab, 0:nnz, :] for ab in range(9)]
        for shift in range(1, nnz):
            same = mine == colsd[shift:shift + nnz, lanes]
            for ab in range(9):
                sums[ab] = sums[ab] + jnp.where(same, blocksd[ab, shift:shift + nnz, :], 0.0)
        for ab in range(9):
            for slot in range(nnz):
                line = jnp.broadcast_to(sums[ab][slot:slot + 1, :], (SUB, LANES))
                wide[ab, slot, :, lanes] = line.astype(BF16)
        return carry

    lax.fori_loop(0, nodes // LANES, widen, 0)

    for chunk in range(own_tiles):
        for a in range(3):
            vr[chunk, a * TILE:(a + 1) * TILE, :] = basis_ref[
                chunk * TILE:(chunk + 1) * TILE, a * width:(a + 1) * width
            ]

    def clear(tile, carry):
        y[tile] = jnp.zeros((3 * TILE, width), F32)
        return carry

    lax.fori_loop(0, own_tiles + ghost_tiles, clear, 0)
    kt_b[...] = jnp.zeros_like(kt_b)

    base = (
        lax.broadcasted_iota(jnp.int32, (4, SUB, LANES), 0) * SUB
        + lax.broadcasted_iota(jnp.int32, (4, SUB, LANES), 1)
    )

    def near_rows(tile, chunk):
        for part in range(TILE // LANES):
            lanes = pl.ds(pl.multiple_of(chunk * TILE + part * LANES, LANES), LANES)
            near = (columns_ref[:, lanes] - tile * TILE).astype(F32)
            for slot in range(nnz):
                rel[part, slot] = jnp.broadcast_to(near[slot:slot + 1, :], (SUB, LANES)).astype(BF16)

    def build_rows(chunk, quarter, part, kt):
        rows = (base + quarter * 4 * SUB).astype(F32).astype(BF16)
        if True:
            lanes = pl.ds(pl.multiple_of(chunk * TILE + part * LANES, LANES), LANES)
            for b in range(3):
                accs = [jnp.zeros((4, SUB, LANES), BF16) for _ in range(3)]
                for slot in range(nnz):
                    hit = jnp.broadcast_to(rel[part, slot][None], (4, SUB, LANES)) == rows
                    for a in range(3):
                        value = jnp.broadcast_to(wide[3 * a + b, slot, :, lanes][None], (4, SUB, LANES))
                        accs[a] = jnp.where(hit, value, accs[a])
                for a in range(3):
                    top = pl.multiple_of(b * TILE + quarter * 4 * SUB, 4 * SUB)
                    left = pl.multiple_of(a * TILE + part * LANES, LANES)
                    kt[pl.ds(top, 4 * SUB), pl.ds(left, LANES)] = accs[a].reshape(4 * SUB, LANES)

    def build_and_multiply(tile, chunk, kt, tile_before, chunk_before, kt_before):
        near_rows(tile, chunk)

        def one(step, carry):
            build_rows(chunk, step // 2, step % 2, kt)
            cut = pl.ds(pl.multiple_of(step * (3 * TILE // 8), 3 * TILE // 8), 3 * TILE // 8)
            y[tile_before, cut, :] += jnp.dot(kt_before[cut, :], vr[chunk_before], preferred_element_type=F32)
            return carry

        lax.fori_loop(0, 8, one, 0)

    def multiply(tile, chunk, kt):
        y[tile] += jnp.dot(kt[...], vr[chunk], preferred_element_type=F32)

    own_pairs = own_tiles // 2
    own_steps = own_tiles * own_pairs
    edge_chunk = (nodes - EDGE) // TILE // 2 * 2
    edge_pairs = (own_tiles - edge_chunk) // 2
    steps = own_steps + ghost_tiles * edge_pairs

    def place(step):
        late = step // own_steps
        tile = (1 - late) * (step // own_pairs) + late * (own_tiles + (step - own_steps) // edge_pairs)
        chunk = (1 - late) * (2 * (step % own_pairs)) + late * (edge_chunk + 2 * (step % edge_pairs))
        return tile, chunk

    def advance(step, carry):
        tile, chunk = place(step)
        tile_before, chunk_before = place((step + steps - 1) % steps)
        build_and_multiply(tile, chunk, kt_a, tile_before, chunk_before + 1, kt_b)
        build_and_multiply(tile, chunk + 1, kt_b, tile, chunk, kt_a)
        return carry

    lax.fori_loop(0, steps, advance, 0)
    tile_last, chunk_last = place(steps - 1)
    multiply(tile_last, chunk_last + 1, kt_b)

    turn = (((0,), (0,)), ((), ()))

    def fold(tile, total):
        return total + lax.dot_general(y[tile].astype(BF16), vr[tile], turn, preferred_element_type=F32)

    total = lax.fori_loop(0, own_tiles, fold, jnp.zeros((width, width), F32))
    for q in range(neighbours):
        ghost_copy(q).wait_recv()
    for tile in range(ghost_tiles):
        for b in range(3):
            total = total + lax.dot_general(
                y[own_tiles + tile, b * TILE:(b + 1) * TILE, :].astype(BF16),
                ghost[tile * TILE:(tile + 1) * TILE, b * width:(b + 1) * width],
                turn,
                preferred_element_type=F32,
            )
    for to in range(n):
        for half in range(2):
            top = (2 * to + half) * half_share
            term4[half, to] = total[top:top + half_share, :]

    pair = pltpu.make_async_remote_copy(
        src_ref=term4.at[other],
        dst_ref=sib,
        send_sem=ssend,
        recv_sem=srecv,
        device_id=(parts_me, me, other),
        device_id_type=MESH,
    )
    pair.start()
    pair.wait_recv()
    summed[...] = term4[grp] + sib[...]

    def share_copy(to, to_grp):
        return pltpu.make_async_remote_copy(
            src_ref=summed.at[to],
            dst_ref=landed.at[grp, me],
            send_sem=rsend.at[to_grp, to],
            recv_sem=rrecv.at[grp, me],
            device_id=(parts_me, to, to_grp),
            device_id_type=MESH,
        )

    def arrival(half, source):
        return pltpu.make_async_remote_copy(
            src_ref=summed.at[source],
            dst_ref=landed.at[half, source],
            send_sem=rsend.at[half, source],
            recv_sem=rrecv.at[half, source],
            device_id=(parts_me, source, half),
            device_id_type=MESH,
        )

    def send(step, carry):
        to = lax.rem(me + step, n)
        share_copy(to, 0).start()
        share_copy(to, 1).start()
        return carry

    lax.fori_loop(1, n, send, 0)
    share_copy(me, other).start()
    landed[grp, me] = summed[me]

    def receive(step, carry):
        source = lax.rem(me + step, n)
        arrival(0, source).wait_recv()
        arrival(1, source).wait_recv()
        return carry

    lax.fori_loop(1, n, receive, 0)
    arrival(other, me).wait_recv()
    for half in range(2):
        out_ref[half * half_share:(half + 1) * half_share, :] = jnp.sum(landed[half], axis=0)

    for q in range(neighbours):
        ghost_copy(q).wait_send()
    pair.wait_send()

    def sent(step, carry):
        to = lax.rem(me + step, n)
        share_copy(to, 0).wait_send()
        share_copy(to, 1).wait_send()
        return carry

    lax.fori_loop(1, n, sent, 0)
    share_copy(me, other).wait_send()


def on_device(basis, blocks, columns, send_list, send_counts):
    nodes, width = basis.shape[0], basis.shape[1] // 3
    nnz = columns.shape[0]
    neighbours, slots = send_list.shape[1], send_list.shape[2]
    n = lax.axis_size("dom")
    share = width // n
    half = share // 2
    own_tiles = nodes // TILE
    ghost_tiles = -(-neighbours * slots // TILE)
    vmem = pl.BlockSpec(memory_space=pltpu.VMEM)
    return pl.pallas_call(
        functools.partial(kernel, n),
        out_shape=jax.ShapeDtypeStruct((share, width), F32),
        in_specs=[vmem, vmem, vmem, vmem, pl.BlockSpec(memory_space=pltpu.SMEM)],
        out_specs=vmem,
        scratch_shapes=[
            pltpu.VMEM((LANES, LANES), F32),
            pltpu.VMEM((neighbours * slots, nodes), BF16),
            pltpu.VMEM((neighbours * slots, 3 * width), BF16),
            pltpu.VMEM((ghost_tiles * TILE, 3 * width), BF16),
            pltpu.VMEM((2 * nnz, nodes), jnp.int32),
            pltpu.VMEM((9, 2 * nnz, LANES), F32),
            pltpu.VMEM((9, nnz, SUB, nodes), BF16),
            pltpu.VMEM((2, nnz, SUB, LANES), BF16),
            pltpu.VMEM((3 * TILE, 3 * TILE), BF16),
            pltpu.VMEM((3 * TILE, 3 * TILE), BF16),
            pltpu.VMEM((own_tiles, 3 * TILE, width), BF16),
            pltpu.VMEM((own_tiles + ghost_tiles, 3 * TILE, width), F32),
            pltpu.VMEM((2, n, half, width), F32),
            pltpu.VMEM((n, half, width), F32),
            pltpu.VMEM((n, half, width), F32),
            pltpu.VMEM((2, n, half, width), F32),
            pltpu.SemaphoreType.DMA((neighbours,)),
            pltpu.SemaphoreType.DMA((neighbours,)),
            pltpu.SemaphoreType.DMA,
            pltpu.SemaphoreType.DMA,
            pltpu.SemaphoreType.DMA((2, n)),
            pltpu.SemaphoreType.DMA((2, n)),
        ],
        compiler_params=pltpu.CompilerParams(
            collective_id=0, has_side_effects=True, vmem_limit_bytes=56 * 1024 * 1024
        ),
    )(basis, blocks, columns, send_list, send_counts)


def solution(mesh):
    in_specs = (
        P(("parts", "dom", "grp"), None),
        P(None, None, ("parts", "dom", "grp")),
        P(None, ("parts", "dom", "grp")),
        P(("parts", "dom", "grp"), None, None),
        P(("parts", "dom", "grp"), None),
    )
    out_specs = P(("parts", "dom"), None)
    return jax.shard_map(
        on_device, mesh=mesh, in_specs=in_specs, out_specs=out_specs, check_vma=False
    )
```
